128 devices in a mesh: row: 8 (over z, core), col: 16 (over y, x).
Axes of the slice: x: 4, y: 4, z: 4, core: 2. Of those that a mesh axis runs over, the one named last changes fastest.
Arguments:
- working: float32 [8, 8, 256, 4, 16, 256], P(None, 'row', None, None, 'col'), may hold values from -6 to 6
- factor_panel: float32 [2, 8, 8, 256, 256], P(None, None, 'row'), may hold values from -0.12 to 2, as said below
Outputs:
- gram_part: float32 [8, 8, 256, 4, 16, 256], P(None, 'row', None, None, 'col')
- finished_columns: float32 [4, 8, 256, 16, 8, 128], P(None, None, None, 'col', 'row')
The draws below stay inside these ranges and needn't reach their ends.
Inputs may be any that keep to these rules, and one draw needn't show every extreme that they name: factor_panel holds a lower-triangular factor: entries above the factor's diagonal are zero and its diagonal entries lie between 1 and 2.
All inputs are finite; a program needn't handle non-finite values.
Results may differ from the reference program's by a relative error of at most 0.0001.
Values sent between devices are 32-bit elements; how exact they have to be, the bound alone decides.
A program may use at most 192 MiB of HBM per device.

```python
import jax
import jax.numpy as jnp
from jax import lax

N = 16384
BLK = 256
K = 30
STEPS = 2
FIN = 32
LR = 8
LC = 4
LF = 4
CW = 128
N_ROW = 8
N_COL = 16


def draw_factor_panel(key, part):
    keys = jax.random.split(jax.random.fold_in(key, 17), 2)
    below = jnp.clip(jax.random.normal(keys[0], (STEPS, N, BLK), jnp.float32) * 0.03, -0.12, 0.12)
    diagonal_values = jax.random.uniform(keys[1], (STEPS, 1, BLK), jnp.float32, 1.0, 2.0)
    row_block = (jnp.arange(N) // BLK)[None, :, None]
    within = (jnp.arange(N) % BLK)[None, :, None]
    column = jnp.arange(BLK)[None, None, :]
    target = (K + jnp.arange(STEPS))[:, None, None]
    inside = jnp.where(within > column, 0.5 * below, jnp.where(within == column, diagonal_values, 0.0))
    values = jnp.where(row_block > target, below, jnp.where(row_block == target, inside, 0.0))
    return values.reshape(STEPS, LR, N // (LR * BLK), BLK, BLK)


def block_scale(stream_key, shape, cuts, smallest, top_value):
    def one(position, blocks):
        draws = jax.random.uniform(jax.random.fold_in(jax.random.fold_in(stream_key, 6), position), (blocks,), jnp.float32, smallest / len(cuts), top_value / len(cuts))
        return jnp.repeat(jnp.exp(draws), shape[position] // blocks).reshape((-1,) + (1,) * (len(shape) - position - 1))

    gain = one(*cuts[0])
    for cut in cuts[1:]:
        gain = gain * one(*cut)
    return gain


def centred(rng, extent, spread, limit, cuts=(), held_as=jnp.bfloat16):
    drawn = jax.random.normal(rng, extent, jnp.float32) * spread
    if len(cuts) > 0:
        drawn = block_scale(rng, extent, cuts, -0.22, 0.18) * drawn
    return jnp.clip(drawn, min=-limit, max=limit).astype(held_as)


def setup_inputs(seed: int = 0) -> dict:
    streams_of = jax.random.split(jax.random.key(seed), 3)
    return {
        "working": centred(streams_of[0], (LR, N_ROW, BLK, LC, N_COL, BLK), 1.0, 6.0, ((1, 8), (4, 16)), jnp.float32),
        "factor_panel": draw_factor_panel(jax.random.fold_in(streams_of[2], 71), 0),
    }


def reference(working, factor_panel):
    matrix = working.reshape(N, N)
    row_block = jnp.arange(N) // BLK
    solved_list = []
    for step_index in range(STEPS):
        target = K + step_index
        column = factor_panel[step_index].reshape(N, BLK)
        diagonal = jnp.tril(column[target * BLK:(target + 1) * BLK])
        solved = lax.linalg.triangular_solve(diagonal, matrix[target * BLK:(target + 1) * BLK], left_side=True, lower=True)
        updated = matrix - jnp.dot(column, solved, precision=lax.Precision.HIGHEST)
        matrix = jnp.where((row_block > target)[:, None], updated, matrix)
        matrix = matrix.at[target * BLK:(target + 1) * BLK].set(solved)
        solved_list.append(solved)
    stacked = jnp.concatenate(solved_list, 0)
    gram = jnp.dot(stacked.T, stacked, precision=lax.Precision.HIGHEST) * (1.0 / (STEPS * BLK))
    gram_part = gram.reshape(LR, N_ROW, BLK, LC, N_COL, BLK)
    finished = matrix[:FIN * BLK].reshape(FIN * BLK, LC, N_COL, BLK).transpose(0, 2, 1, 3)
    finished_columns = finished.reshape(LF, N_ROW, BLK, N_COL, N_ROW, CW)
    return (gram_part, finished_columns)
```

```python
import jax
import jax.numpy as jnp
from jax import lax
from jax.experimental import pallas as pl
from jax.experimental.pallas import tpu as pltpu
from jax.sharding import PartitionSpec as P

MESH = pl.DeviceIdType.MESH
F32 = jnp.float32
BF16 = jnp.bfloat16
BLK = 256
HALF = 128
NJ = 4
SLOT = 3
SCALE = 1.0 / 512


def full(a, b):
    return lax.dot_general(
        a, b, (((1,), (0,)), ((), ())), precision=lax.Precision.HIGHEST, preferred_element_type=F32
    )


def small_inverse(block):
    row = lax.broadcasted_iota(jnp.int32, (HALF, HALF), 0)
    col = lax.broadcasted_iota(jnp.int32, (HALF, HALF), 1)
    eye = row == col
    on_diagonal = jnp.where(eye, block, 0.0)
    inv_col = 1.0 / jnp.sum(on_diagonal, axis=1, keepdims=True)
    inv_row = 1.0 / jnp.sum(on_diagonal, axis=0, keepdims=True)
    first = (row == col + 1) & ((row & 1) == 1)
    inverse = jnp.where(eye, inv_col, jnp.where(first, -block * inv_col * inv_row, 0.0))
    shift = 1
    while (1 << shift) < HALF:
        below = ((row >> shift) & 1) == 1
        beside = (col >> shift) == (row >> shift) - 1
        lower = jnp.where(below & beside, block, 0.0)
        inverse = inverse - full(inverse, full(lower, inverse))
        shift += 1
    return inverse


def split(value):
    high = value.astype(BF16)
    low = (value - high.astype(F32)).astype(BF16)
    return high, low


def tdot(a, b):
    return lax.dot_general(a, b, (((0,), (0,)), ((), ())), preferred_element_type=F32)


def kernel(
    w_ref, f_ref, gram_ref, fin_ref,
    own, oth, panel, cross, high, low, stage, slab, diag, lower, inv,
    load_sem, a2a_send, a2a_recv, a2b_send, a2b_recv, local_sem,
    oth_send, oth_recv, own_send, own_recv, copy_sem,
    dir_send, panel_recv, cross_send, cross_recv, stage_sem,
):
    r = lax.axis_index("row")
    c = lax.axis_index("col")
    z, k = lax.div(r, 2), lax.rem(r, 2)
    y, x = lax.div(c, 4), lax.rem(c, 4)
    dx = lax.rem(x + 4 - 2 * lax.rem(z, 2), 4)
    dy = lax.rem(y + 4 - lax.div(z, 2), 4)
    other = (r + 1 - 2 * k, c)
    right = (r, 4 * y + lax.rem(x + 1, 4))
    left = (r, 4 * y + lax.rem(x + 3, 4))
    up = (r, 4 * lax.rem(y + 1, 4) + x)
    down = (r, 4 * lax.rem(y + 3, 4) + x)
    is_top = z == 3
    is_source = lax.div(lax.rem(c, 8), 2) == z
    source_panel = 2 * lax.rem(c, 2) + lax.div(c, 8)

    def remote(src, dst, send, recv, device):
        return pltpu.make_async_remote_copy(
            src, dst, send, recv, device_id=device, device_id_type=MESH
        )

    def loads():
        found = [pltpu.make_async_copy(f_ref.at[k, SLOT, 0], diag, load_sem.at[8])]
        found.append(pltpu.make_async_copy(f_ref.at[0, SLOT, 0], lower, load_sem.at[9]))
        for s in range(8):
            found.append(
                pltpu.make_async_copy(
                    w_ref.at[SLOT, :, s, 0, :], slab.at[s // 2, s % 2], load_sem.at[s]
                )
            )
        return found

    @pl.when(is_top)
    def _():
        for copy in loads():
            copy.start()

    barrier = pltpu.get_barrier_semaphore()
    for d in range(1, 8):
        pl.semaphore_signal(
            barrier, inc=1, device_id=(lax.rem(r + d, 8), c), device_id_type=MESH
        )
    for device in (right, left, up, down):
        pl.semaphore_signal(barrier, inc=1, device_id=device, device_id_type=MESH)
    pl.semaphore_wait(barrier, 11)

    def partner(d):
        return 2 * (z ^ (d >> 1)) + (k ^ (d & 1))

    def finished(d):
        t = partner(d)
        return remote(
            w_ref.at[pl.ds(0, 3), :, t],
            fin_ref.at[pl.ds(0, 3), r],
            a2a_send.at[d], a2a_recv.at[d], (t, c),
        )

    def finished_last(d):
        t = partner(d)
        return remote(
            w_ref.at[pl.ds(3, 1), :, t],
            fin_ref.at[pl.ds(3, 1), r],
            a2b_send.at[d], a2b_recv.at[d], (t, c),
        )

    for d in range(1, 8):
        finished(d).start()

        @pl.when(z < 3)
        def _():
            finished_last(d).start()

    own_rows = pltpu.make_async_copy(
        w_ref.at[pl.ds(0, 3), :, r], fin_ref.at[pl.ds(0, 3), r], local_sem.at[0]
    )
    own_last = pltpu.make_async_copy(
        w_ref.at[pl.ds(3, 1), :, r], fin_ref.at[pl.ds(3, 1), r], local_sem.at[1]
    )
    own_rows.start()

    @pl.when(z < 3)
    def _():
        own_last.start()

    @pl.when(is_top)
    def _():
        for copy in loads():
            copy.wait()
        top = small_inverse(diag[0:HALF, 0:HALF])
        bottom = small_inverse(diag[HALF:BLK, HALF:BLK])
        inv[0:HALF, 0:HALF] = top
        inv[0:HALF, HALF:BLK] = jnp.zeros((HALF, HALF), F32)
        inv[HALF:BLK, HALF:BLK] = bottom
        inv[HALF:BLK, 0:HALF] = -full(bottom, full(diag[HALF:BLK, 0:HALF], top))

    def to_other(j):
        return remote(own.at[j], oth.at[j], oth_send.at[j], oth_recv.at[j], other)

    def down_ring(j, target, sem):
        return remote(
            own.at[j], own.at[j], own_send.at[sem, j], own_recv.at[j], (2 * target + k, c)
        )

    def forwards_ring(j):
        return ((z == 0) & (j < 2)) | ((z == 2) & (j >= 2))

    def to_panel(j):
        return pltpu.make_async_copy(own.at[j], panel.at[source_panel, j], copy_sem.at[j])

    def solved_chunk(j):
        @pl.when(is_top)
        def _():
            @pl.when(k == 1)
            def _():
                to_other(j).wait_recv()
                for h in range(2):
                    slab[j, h] = slab[j, h] - full(lower[...], oth[j, h])

            for h in range(2):
                own[j, h] = full(inv[...], slab[j, h])

        @pl.when(z < 3)
        def _():
            down_ring(j, 1, 0).wait_recv()

        @pl.when(is_source)
        def _():
            to_panel(j).start()

        to_other(j).start()

        @pl.when(is_top)
        def _():
            down_ring(j, 0, 0).start()
            down_ring(j, 2, 1).start()

        @pl.when(forwards_ring(j))
        def _():
            down_ring(j, 1, 0).start()

        @pl.when(is_source)
        def _():
            to_panel(j).wait()

    near_x = ((dx == 1) | (dx == 2)).astype(jnp.int32)
    near_y = (dy == 2).astype(jnp.int32)

    def which(n):
        low_bit, high_bit = n & 1, n >> 1
        kp = jnp.where(k == 0, low_bit, high_bit) ^ near_x
        b = jnp.where(k == 0, high_bit, low_bit) ^ near_y
        return kp, b

    def hops(kp, b, j):
        p = 2 * kp + b
        odd = lax.rem(kp + j, 2)
        x_active = (k == 1) | (dy == 2 * b)
        y_active = (k == 0) | (dx == kp)
        goes = (
            x_active & ((dx == kp) | ((kp == 1) & (dx == 2))),
            x_active & ((dx == kp) | ((kp == 0) & (dx == 3))),
            y_active
            & (
                (dy == 2 * b)
                | ((odd == 0) & (dy == 1) & (b == 0))
                | ((odd == 1) & (dy == 3) & (b == 1))
            ),
            y_active
            & (
                (dy == 2 * b)
                | ((odd == 0) & (dy == 1) & (b == 1))
                | ((odd == 1) & (dy == 3) & (b == 0))
            ),
        )
        return [
            (
                go,
                remote(
                    panel.at[p, j], panel.at[p, j], dir_send.at[i, p, j], panel_recv.at[p, j], device
                ),
            )
            for i, (go, device) in enumerate(zip(goes, (right, left, up, down)))
        ]

    def to_cross(b, j):
        return remote(
            panel.at[2 * (1 - k) + b, j], cross.at[b, j], cross_send.at[b, j], cross_recv.at[b, j], other
        )

    def pass_on(n, j):
        kp, b = which(n)
        p = 2 * kp + b
        copies = hops(kp, b, j)

        @pl.when(jnp.logical_not(is_source & (source_panel == p)))
        def _():
            copies[0][1].wait_recv()

        for go, copy in copies:
            @pl.when(go)
            def _(copy=copy):
                copy.start()

        @pl.when(kp != k)
        def _():
            to_cross(b, j).start()

    def staged(i, s):
        slot = i & 1
        return pltpu.make_async_copy(
            stage.at[slot, s], gram_ref.at[i, :, s, 0, :], stage_sem.at[slot, s]
        )

    def split_columns():
        for j in range(NJ):
            @pl.when(jnp.logical_not(is_top & (k == 1)))
            def _(j=j):
                to_other(j).wait_recv()
            for h in range(2):
                s = 2 * j + h
                at = slice(HALF * s, HALF * (s + 1))
                high[0:BLK, at], low[0:BLK, at] = split(own[j, h])
                high[BLK:, at], low[BLK:, at] = split(oth[j, h])

    def gram_block(j, b):
        i = 2 * j + b
        to_cross(b, j).wait_recv()
        p = 2 * k + b
        mine = jnp.concatenate([panel[p, j, 0], panel[p, j, 1]], axis=1)
        theirs = jnp.concatenate([cross[b, j, 0], cross[b, j, 1]], axis=1)
        a_high, a_low = split(jnp.concatenate([mine, theirs], axis=0))

        @pl.when(i >= 2)
        def _():
            for s in range(8):
                staged(i, s).wait()

        for q in range(4):
            at = slice(BLK * q, BLK * (q + 1))
            b_high, b_low = high[:, at], low[:, at]
            value = (tdot(a_low, b_high) + tdot(a_high, b_low)) + tdot(a_high, b_high)
            value = value * SCALE
            stage[i & 1, 2 * q] = value[:, :HALF]
            stage[i & 1, 2 * q + 1] = value[:, HALF:]
            staged(i, 2 * q).start()
            staged(i, 2 * q + 1).start()

    def step(t, carry):
        @pl.when(t < 4)
        def _():
            solved_chunk(t)
            pass_on(0, t)
            pass_on(1, t)

        @pl.when((t >= 1) & (t < 5))
        def _():
            pass_on(2, t - 1)
            pass_on(3, t - 1)

        return carry

    lax.fori_loop(0, 5, step, 0)

    split_columns()
    last = [
        pltpu.make_async_copy(
            own.at[lax.div(r, 2), lax.rem(r, 2)], fin_ref.at[SLOT, 6 + k, :, 0, :], local_sem.at[2]
        ),
        pltpu.make_async_copy(
            oth.at[lax.div(r, 2), lax.rem(r, 2)], fin_ref.at[SLOT, 7 - k, :, 0, :], local_sem.at[3]
        ),
    ]
    for copy in last:
        copy.start()

    def product(j, carry):
        gram_block(j, 0)
        gram_block(j, 1)
        return carry

    lax.fori_loop(0, NJ, product, 0)

    for i in (6, 7):
        for s in range(8):
            staged(i, s).wait()
    for copy in last:
        copy.wait()
    own_rows.wait()

    @pl.when(z < 3)
    def _():
        own_last.wait()

    def close(j, carry):
        to_other(j).wait_send()

        @pl.when(is_top)
        def _():
            down_ring(j, 0, 0).wait_send()
            down_ring(j, 2, 1).wait_send()

        @pl.when(forwards_ring(j))
        def _():
            down_ring(j, 1, 0).wait_send()

        for kp in range(2):
            for b in range(2):
                for go, copy in hops(kp, b, j):
                    @pl.when(go)
                    def _(copy=copy):
                        copy.wait_send()
        for b in range(2):
            to_cross(b, j).wait_send()
        return carry

    lax.fori_loop(0, NJ, close, 0)
    for d in range(1, 8):
        finished(d).wait()

        @pl.when(z < 3)
        def _():
            finished_last(d).wait_send()

        @pl.when(partner(d) < 6)
        def _():
            finished_last(d).wait_recv()


def per_device(working, factor_panel):
    dma = pltpu.SemaphoreType.DMA
    gram, finished = pl.pallas_call(
        kernel,
        out_shape=[
            pltpu.VMEM((8, BLK, 8, 1, HALF), F32),
            pltpu.VMEM((4, 8, BLK, 1, HALF), F32),
        ],
        in_specs=[pl.BlockSpec(memory_space=pl.ANY)] * 2,
        out_specs=[pl.BlockSpec(memory_space=pltpu.VMEM)] * 2,
        scratch_shapes=[
            pltpu.VMEM((NJ, 2, BLK, HALF), F32),
            pltpu.VMEM((NJ, 2, BLK, HALF), F32),
            pltpu.VMEM((4, NJ, 2, BLK, HALF), F32),
            pltpu.VMEM((2, NJ, 2, BLK, HALF), F32),
            pltpu.VMEM((2 * BLK, 8 * HALF), BF16),
            pltpu.VMEM((2 * BLK, 8 * HALF), BF16),
            pltpu.VMEM((2, 8, BLK, HALF), F32),
            pltpu.VMEM((NJ, 2, BLK, HALF), F32),
            pltpu.VMEM((BLK, BLK), F32),
            pltpu.VMEM((BLK, BLK), F32),
            pltpu.VMEM((BLK, BLK), F32),
            dma((10,)),
            dma((8,)), dma((8,)), dma((8,)), dma((8,)),
            dma((4,)),
            dma((NJ,)), dma((NJ,)),
            dma((2, NJ)), dma((NJ,)),
            dma((NJ,)),
            dma((4, 4, NJ)), dma((4, NJ)),
            dma((2, NJ)), dma((2, NJ)),
            dma((2, 8)),
        ],
        compiler_params=pltpu.CompilerParams(
            collective_id=0, has_side_effects=True, vmem_limit_bytes=44 * 2**20
        ),
        cost_estimate=pl.CostEstimate(
            flops=3 * 2**31, bytes_accessed=20 * 2**20, transcendentals=0
        ),
        name="window",
    )(working.reshape(8, BLK, 8, 1, HALF), factor_panel)
    return gram.reshape(8, 1, BLK, 4, 1, BLK), finished.reshape(4, 8, BLK, 1, 1, HALF)


def solution(mesh):
    placed = (P(None, "row", None, None, "col", None), P(None, None, "row", None, None))
    return jax.shard_map(
        per_device,
        mesh=mesh,
        in_specs=placed,
        out_specs=(
            P(None, "row", None, None, "col", None),
            P(None, None, None, "col", "row", None),
        ),
        check_vma=False,
    )
```

```python
import jax
import jax.numpy as jnp
from jax import lax
from jax.experimental import pallas as pl
from jax.experimental.pallas import tpu as pltpu
from jax.sharding import PartitionSpec as P

MESH = pl.DeviceIdType.MESH
F32 = jnp.float32
BF16 = jnp.bfloat16
BLK = 256
HALF = 128
PARTS = 1
ROWS = BLK // PARTS
NQ = 8 * PARTS
LAG = 2
STEPS = NQ + 4 * LAG
EARLY = 0
AFTER = NQ
PACE = 28
SLOT = 3
SCALE = 1.0 / 512


def full(a, b):
    return lax.dot_general(
        a, b, (((1,), (0,)), ((), ())), precision=lax.Precision.HIGHEST, preferred_element_type=F32
    )


def small_inverse(block):
    row = lax.broadcasted_iota(jnp.int32, (HALF, HALF), 0)
    col = lax.broadcasted_iota(jnp.int32, (HALF, HALF), 1)
    eye = row == col
    on_diagonal = jnp.where(eye, block, 0.0)
    inv_col = 1.0 / jnp.sum(on_diagonal, axis=1, keepdims=True)
    inv_row = 1.0 / jnp.sum(on_diagonal, axis=0, keepdims=True)
    first = (row == col + 1) & ((row & 1) == 1)
    inverse = jnp.where(eye, inv_col, jnp.where(first, -block * inv_col * inv_row, 0.0))
    shift = 1
    while (1 << shift) < HALF:
        below = ((row >> shift) & 1) == 1
        beside = (col >> shift) == (row >> shift) - 1
        lower = jnp.where(below & beside, block, 0.0)
        inverse = inverse - full(inverse, full(lower, inverse))
        shift += 1
    return inverse


def split(value):
    high = value.astype(BF16)
    low = (value - high.astype(F32)).astype(BF16)
    return high, low


def tdot(a, b):
    return lax.dot_general(a, b, (((0,), (0,)), ((), ())), preferred_element_type=F32)


def kernel(
    w_ref, f_ref, gram_ref, fin_ref,
    own, oth, panel, cross, high, low, stage, slab, diag, lower, inv,
    load_sem, a2a_send, a2a_recv, local_sem,
    oth_send, oth_recv, own_send, own_recv, copy_sem,
    dir_send, panel_recv, cross_send, cross_recv, stage_sem,
):
    r = lax.axis_index("row")
    c = lax.axis_index("col")
    z, k = lax.div(r, 2), lax.rem(r, 2)
    y, x = lax.div(c, 4), lax.rem(c, 4)
    dx = lax.rem(x + 4 - 2 * lax.rem(z, 2), 4)
    dy = lax.rem(y + 4 - lax.div(z, 2), 4)
    other = (r + 1 - 2 * k, c)
    right = (r, 4 * y + lax.rem(x + 1, 4))
    left = (r, 4 * y + lax.rem(x + 3, 4))
    up = (r, 4 * lax.rem(y + 1, 4) + x)
    down = (r, 4 * lax.rem(y + 3, 4) + x)
    is_top = z == 3
    is_source = lax.div(lax.rem(c, 8), 2) == z
    source_panel = 2 * lax.rem(c, 2) + lax.div(c, 8)

    def remote(src, dst, send, recv, device):
        return pltpu.make_async_remote_copy(
            src, dst, send, recv, device_id=device, device_id_type=MESH
        )

    def loads():
        found = [pltpu.make_async_copy(f_ref.at[k, SLOT, 0], diag, load_sem.at[8])]
        found.append(pltpu.make_async_copy(f_ref.at[0, SLOT, 0], lower, load_sem.at[9]))
        for s in range(8):
            found.append(
                pltpu.make_async_copy(
                    w_ref.at[SLOT, :, s, 0, :], slab.at[s], load_sem.at[s]
                )
            )
        return found

    @pl.when(is_top)
    def _():
        for copy in loads():
            copy.start()

    barrier = pltpu.get_barrier_semaphore()
    for d in range(1, 8):
        pl.semaphore_signal(
            barrier, inc=1, device_id=(lax.rem(r + d, 8), c), device_id_type=MESH
        )
    for device in (right, left, up, down):
        pl.semaphore_signal(barrier, inc=1, device_id=device, device_id_type=MESH)
    pl.semaphore_wait(barrier, 11)

    def finished(m, source):
        d, f = 1 + lax.rem(m, 7), lax.div(m, 7)
        t = r ^ d
        origin = t if source else r
        return (
            (f < SLOT) | (origin < 6),
            remote(
                w_ref.at[f, :, t], fin_ref.at[f, r], a2a_send.at[m], a2a_recv.at[m], (t, c)
            ),
        )

    def start_finished(m, early):
        go, copy = finished(m, False)
        d = 1 + lax.rem(m, 7)
        free = (z == 1) | (lax.div(r ^ d, 2) == 3) | (d == 1) | (m < EARLY)

        @pl.when(go & (free if early else jnp.logical_not(free)))
        def _():
            copy.start()

    def start_early(m, carry):
        start_finished(m, True)
        return carry

    lax.fori_loop(0, 28, start_early, 0)

    own_rows = pltpu.make_async_copy(
        w_ref.at[pl.ds(0, 3), :, r], fin_ref.at[pl.ds(0, 3), r], local_sem.at[0]
    )
    own_last = pltpu.make_async_copy(
        w_ref.at[pl.ds(3, 1), :, r], fin_ref.at[pl.ds(3, 1), r], local_sem.at[1]
    )
    own_rows.start()

    @pl.when(z < 3)
    def _():
        own_last.start()

    @pl.when(is_top)
    def _():
        for copy in loads():
            copy.wait()
        top = small_inverse(diag[0:HALF, 0:HALF])
        bottom = small_inverse(diag[HALF:BLK, HALF:BLK])
        inv[0:HALF, 0:HALF] = top
        inv[0:HALF, HALF:BLK] = jnp.zeros((HALF, HALF), F32)
        inv[HALF:BLK, HALF:BLK] = bottom
        inv[HALF:BLK, 0:HALF] = -full(bottom, full(diag[HALF:BLK, 0:HALF], top))

    def part(ref, q):
        if PARTS == 1:
            return ref.at[q]
        return ref.at[lax.div(q, PARTS), pl.ds(pl.multiple_of(lax.rem(q, PARTS) * ROWS, ROWS), ROWS), :]

    def to_other(q):
        return remote(part(own, q), part(oth, q), oth_send.at[q], oth_recv.at[q], other)

    def down_ring(q, target, sem):
        return remote(
            part(own, q), part(own, q), own_send.at[sem, q], own_recv.at[q], (2 * target + k, c)
        )

    def forwards_ring(q):
        return ((z == 0) & (lax.rem(q, 2) == 0)) | ((z == 2) & (lax.rem(q, 2) == 1))

    def to_panel(q):
        return pltpu.make_async_copy(part(own, q), part(panel.at[source_panel], q), copy_sem.at[q])

    def solved_chunk(q):
        @pl.when(is_top)
        def _():
            @pl.when(k == 1)
            def _():
                to_other(q).wait_recv()

            @pl.when(lax.rem(q, PARTS) == PARTS - 1)
            def _():
                s = lax.div(q, PARTS)

                @pl.when(k == 1)
                def _():
                    slab[s] = slab[s] - full(lower[...], oth[s])

                own[s] = full(inv[...], slab[s])

        @pl.when(z < 3)
        def _():
            down_ring(q, 1, 0).wait_recv()

    def send_solved(q):
        @pl.when(is_source)
        def _():
            to_panel(q).start()

        to_other(q).start()

        @pl.when(is_top)
        def _():
            down_ring(q, 0, 0).start()
            down_ring(q, 2, 1).start()

        @pl.when(forwards_ring(q))
        def _():
            down_ring(q, 1, 0).start()

    def hops(kp, b, q):
        odd = lax.rem(kp + q, 2)
        x_active = (k == 1) | (dy == 2 * b)
        y_active = (k == 0) | (dx == kp)
        return (
            (x_active & ((dx == kp) | ((kp == 1) & (dx == 2))), right),
            (x_active & ((dx == kp) | ((kp == 0) & (dx == 3))), left),
            (
                y_active
                & (
                    (dy == 2 * b)
                    | ((odd == 0) & (dy == 1) & (b == 0))
                    | ((odd == 1) & (dy == 3) & (b == 1))
                ),
                up,
            ),
            (
                y_active
                & (
                    (dy == 2 * b)
                    | ((odd == 0) & (dy == 1) & (b == 1))
                    | ((odd == 1) & (dy == 3) & (b == 0))
                ),
                down,
            ),
        )

    def hop(src, p, q, i, device):
        return remote(
            part(src, q), part(panel.at[p], q), dir_send.at[i, p, q], panel_recv.at[p, q], device
        )

    def to_cross(src, b, q):
        return remote(
            part(src, q), part(cross.at[b], q), cross_send.at[b, q], cross_recv.at[b, q], other
        )

    def start_all(src, kp, b, q):
        for i, (go, device) in enumerate(hops(kp, b, q)):
            @pl.when(go)
            def _(i=i, device=device):
                hop(src, 2 * kp + b, q, i, device).start()

        @pl.when(kp != k)
        def _():
            to_cross(src, b, q).start()

    def distance(kp, b):
        ex = lax.rem(dx + 4 - kp, 4)
        ey = lax.rem(dy + 4 - 2 * b, 4)
        return jnp.minimum(ex, 4 - ex) + jnp.minimum(ey, 4 - ey)

    def pass_on(kp, b, t):
        far = distance(kp, b)
        q = t - LAG * far

        @pl.when((far > 0) & (q >= 0) & (q < NQ))
        def _():
            p = 2 * kp + b
            hop(panel.at[p], p, q, 0, right).wait_recv()
            start_all(panel.at[p], kp, b, q)

    def staged(i, s):
        slot = i & 1
        return pltpu.make_async_copy(
            stage.at[slot, s], gram_ref.at[i, :, s, 0, :], stage_sem.at[slot, s]
        )

    def split_columns():
        @pl.when(jnp.logical_not(is_top & (k == 1)))
        def _():
            for q in range(NQ):
                to_other(q).wait_recv()

        for s in range(8):
            at = slice(HALF * s, HALF * (s + 1))
            high[0:BLK, at], low[0:BLK, at] = split(own[s])
            high[BLK:, at], low[BLK:, at] = split(oth[s])

    def gram_block(j, b):
        i = 2 * j + b
        p = 2 * k + b
        for n in range(2 * PARTS):
            to_cross(own, b, 2 * PARTS * j + n).wait_recv()
        mine = jnp.concatenate([panel[p, 2 * j], panel[p, 2 * j + 1]], axis=1)
        theirs = jnp.concatenate([cross[b, 2 * j], cross[b, 2 * j + 1]], axis=1)
        a_high, a_low = split(jnp.concatenate([mine, theirs], axis=0))

        @pl.when(i >= 2)
        def _():
            for s in range(8):
                staged(i, s).wait()

        for q in range(4):
            at = slice(BLK * q, BLK * (q + 1))
            b_high, b_low = high[:, at], low[:, at]
            value = (tdot(a_low, b_high) + tdot(a_high, b_low)) + tdot(a_high, b_high)
            value = value * SCALE
            stage[i & 1, 2 * q] = value[:, :HALF]
            stage[i & 1, 2 * q + 1] = value[:, HALF:]
            staged(i, 2 * q).start()
            staged(i, 2 * q + 1).start()

    def step(t, carry):
        @pl.when(t < NQ)
        def _():
            solved_chunk(t)

            @pl.when(is_source)
            def _():
                start_all(own, lax.rem(c, 2), lax.div(c, 8), t)

            send_solved(t)

        for kp in range(2):
            for b in range(2):
                pass_on(kp, b, t)

        def start_late(m, carry):
            start_finished(m, False)
            return carry

        first = EARLY + PACE * (t - AFTER)
        lax.fori_loop(
            jnp.where(t < AFTER, 28, jnp.minimum(first, 28)),
            jnp.where(t == STEPS - 1, 28, jnp.minimum(first + PACE, 28)),
            start_late,
            0,
        )
        return carry

    lax.fori_loop(0, STEPS, step, 0)

    @pl.when(is_source)
    def _():
        for q in range(NQ):
            to_panel(q).wait()

    split_columns()
    last = [
        pltpu.make_async_copy(
            own.at[r], fin_ref.at[SLOT, 6 + k, :, 0, :], local_sem.at[2]
        ),
        pltpu.make_async_copy(
            oth.at[r], fin_ref.at[SLOT, 7 - k, :, 0, :], local_sem.at[3]
        ),
    ]
    for copy in last:
        copy.start()

    def product(j, carry):
        gram_block(j, 0)
        gram_block(j, 1)
        return carry

    lax.fori_loop(0, 4, product, 0)

    for i in (6, 7):
        for s in range(8):
            staged(i, s).wait()
    for copy in last:
        copy.wait()
    own_rows.wait()

    @pl.when(z < 3)
    def _():
        own_last.wait()

    def close(q, carry):
        to_other(q).wait_send()

        @pl.when(is_top)
        def _():
            down_ring(q, 0, 0).wait_send()
            down_ring(q, 2, 1).wait_send()

        @pl.when(forwards_ring(q))
        def _():
            down_ring(q, 1, 0).wait_send()

        for kp in range(2):
            for b in range(2):
                for i, (go, device) in enumerate(hops(kp, b, q)):
                    @pl.when(go)
                    def _(i=i, p=2 * kp + b, device=device):
                        hop(panel.at[p], p, q, i, device).wait_send()
        for b in range(2):
            to_cross(own, b, q).wait_send()
        return carry

    lax.fori_loop(0, NQ, close, 0)

    def close_finished(m, carry):
        go, copy = finished(m, False)

        @pl.when(go)
        def _():
            copy.wait_send()

        go, copy = finished(m, True)

        @pl.when(go)
        def _():
            copy.wait_recv()

        return carry

    lax.fori_loop(0, 28, close_finished, 0)


def per_device(working, factor_panel):
    dma = pltpu.SemaphoreType.DMA
    gram, finished = pl.pallas_call(
        kernel,
        out_shape=[
            pltpu.VMEM((8, BLK, 8, 1, HALF), F32),
            pltpu.VMEM((4, 8, BLK, 1, HALF), F32),
        ],
        in_specs=[pl.BlockSpec(memory_space=pl.ANY)] * 2,
        out_specs=[pl.BlockSpec(memory_space=pltpu.VMEM)] * 2,
        scratch_shapes=[
            pltpu.VMEM((8, BLK, HALF), F32),
            pltpu.VMEM((8, BLK, HALF), F32),
            pltpu.VMEM((4, 8, BLK, HALF), F32),
            pltpu.VMEM((2, 8, BLK, HALF), F32),
            pltpu.VMEM((2 * BLK, 8 * HALF), BF16),
            pltpu.VMEM((2 * BLK, 8 * HALF), BF16),
            pltpu.VMEM((2, 8, BLK, HALF), F32),
            pltpu.VMEM((8, BLK, HALF), F32),
            pltpu.VMEM((BLK, BLK), F32),
            pltpu.VMEM((BLK, BLK), F32),
            pltpu.VMEM((BLK, BLK), F32),
            dma((10,)),
            dma((28,)), dma((28,)),
            dma((4,)),
            dma((NQ,)), dma((NQ,)),
            dma((2, NQ)), dma((NQ,)),
            dma((NQ,)),
            dma((4, 4, NQ)), dma((4, NQ)),
            dma((2, NQ)), dma((2, NQ)),
            dma((2, 8)),
        ],
        compiler_params=pltpu.CompilerParams(
            collective_id=0, has_side_effects=True, vmem_limit_bytes=44 * 2**20
        ),
        cost_estimate=pl.CostEstimate(
            flops=3 * 2**31, bytes_accessed=20 * 2**20, transcendentals=0
        ),
        name="window",
    )(working.reshape(8, BLK, 8, 1, HALF), factor_panel)
    return gram.reshape(8, 1, BLK, 4, 1, BLK), finished.reshape(4, 8, BLK, 1, 1, HALF)


def solution(mesh):
    placed = (P(None, "row", None, None, "col", None), P(None, None, "row", None, None))
    return jax.shard_map(
        per_device,
        mesh=mesh,
        in_specs=placed,
        out_specs=(
            P(None, "row", None, None, "col", None),
            P(None, None, None, "col", "row", None),
        ),
        check_vma=False,
    )
```

```python
import jax
import jax.numpy as jnp
from jax import lax
from jax.experimental import pallas as pl
from jax.experimental.pallas import tpu as pltpu
from jax.sharding import PartitionSpec as P

MESH = pl.DeviceIdType.MESH
F32 = jnp.float32
BF16 = jnp.bfloat16
BLK = 256
HALF = 128
PARTS = 1
ROWS = BLK // PARTS
NQ = 8 * PARTS
LAG = 2
STEPS = NQ + 4 * LAG
EARLY = 0
AFTER = NQ
PACE = 28
SLOT = 3
SCALE = 1.0 / 512


def full(a, b):
    return lax.dot_general(
        a, b, (((1,), (0,)), ((), ())), precision=lax.Precision.HIGHEST, preferred_element_type=F32
    )


def small_inverse(block):
    row = lax.broadcasted_iota(jnp.int32, (HALF, HALF), 0)
    col = lax.broadcasted_iota(jnp.int32, (HALF, HALF), 1)
    eye = row == col
    on_diagonal = jnp.where(eye, block, 0.0)
    inv_col = 1.0 / jnp.sum(on_diagonal, axis=1, keepdims=True)
    inv_row = 1.0 / jnp.sum(on_diagonal, axis=0, keepdims=True)
    first = (row == col + 1) & ((row & 1) == 1)
    inverse = jnp.where(eye, inv_col, jnp.where(first, -block * inv_col * inv_row, 0.0))
    shift = 1
    while (1 << shift) < HALF:
        below = ((row >> shift) & 1) == 1
        beside = (col >> shift) == (row >> shift) - 1
        lower = jnp.where(below & beside, block, 0.0)
        inverse = inverse - full(inverse, full(lower, inverse))
        shift += 1
    return inverse


def split(value):
    high = value.astype(BF16)
    low = (value - high.astype(F32)).astype(BF16)
    return high, low


def tdot(a, b):
    return lax.dot_general(a, b, (((0,), (0,)), ((), ())), preferred_element_type=F32)


def kernel(
    w_ref, f_ref, gram_ref, fin_ref,
    own, oth, panel, cross, high, low, stage, slab, diag, lower, inv,
    load_sem, a2a_send, a2a_recv, local_sem,
    oth_send, oth_recv, own_send, own_recv, copy_sem,
    dir_send, panel_recv, cross_send, cross_recv, stage_sem,
):
    r = lax.axis_index("row")
    c = lax.axis_index("col")
    z, k = lax.div(r, 2), lax.rem(r, 2)
    y, x = lax.div(c, 4), lax.rem(c, 4)
    dx = lax.rem(x + 4 - 2 * lax.rem(z, 2), 4)
    dy = lax.rem(y + 4 - lax.div(z, 2), 4)
    other = (r + 1 - 2 * k, c)
    right = (r, 4 * y + lax.rem(x + 1, 4))
    left = (r, 4 * y + lax.rem(x + 3, 4))
    up = (r, 4 * lax.rem(y + 1, 4) + x)
    down = (r, 4 * lax.rem(y + 3, 4) + x)
    is_top = z == 3
    is_source = lax.div(lax.rem(c, 8), 2) == z
    source_panel = 2 * lax.rem(c, 2) + lax.div(c, 8)

    def remote(src, dst, send, recv, device):
        return pltpu.make_async_remote_copy(
            src, dst, send, recv, device_id=device, device_id_type=MESH
        )

    def loads():
        found = [pltpu.make_async_copy(f_ref.at[k, SLOT, 0], diag, load_sem.at[8])]
        found.append(pltpu.make_async_copy(f_ref.at[0, SLOT, 0], lower, load_sem.at[9]))
        for s in range(8):
            found.append(
                pltpu.make_async_copy(
                    w_ref.at[SLOT, :, s, 0, :], slab.at[s], load_sem.at[s]
                )
            )
        return found

    @pl.when(is_top)
    def _():
        for copy in loads():
            copy.start()

    barrier = pltpu.get_barrier_semaphore()
    for d in range(1, 8):
        pl.semaphore_signal(
            barrier, inc=1, device_id=(lax.rem(r + d, 8), c), device_id_type=MESH
        )
    for device in (right, left, up, down):
        pl.semaphore_signal(barrier, inc=1, device_id=device, device_id_type=MESH)
    pl.semaphore_wait(barrier, 11)

    def finished(m, source):
        d, f = 1 + lax.rem(m + 3, 7), lax.div(m, 7)
        t = r ^ d
        origin = t if source else r
        return (
            (f < SLOT) | (origin < 6),
            remote(
                w_ref.at[f, :, t], fin_ref.at[f, r], a2a_send.at[m], a2a_recv.at[m], (t, c)
            ),
        )

    def start_finished(m, early):
        go, copy = finished(m, False)
        d = 1 + lax.rem(m + 3, 7)
        free = (z == 1) | (lax.div(r ^ d, 2) == 3) | (d == 1) | (m < EARLY)

        @pl.when(go & (free if early else jnp.logical_not(free)))
        def _():
            copy.start()

    def start_early(m, carry):
        start_finished(m, True)
        return carry

    lax.fori_loop(0, 28, start_early, 0)

    own_rows = pltpu.make_async_copy(
        w_ref.at[pl.ds(0, 3), :, r], fin_ref.at[pl.ds(0, 3), r], local_sem.at[0]
    )
    own_last = pltpu.make_async_copy(
        w_ref.at[pl.ds(3, 1), :, r], fin_ref.at[pl.ds(3, 1), r], local_sem.at[1]
    )
    own_rows.start()

    @pl.when(z < 3)
    def _():
        own_last.start()

    @pl.when(is_top)
    def _():
        for copy in loads():
            copy.wait()
        top = small_inverse(diag[0:HALF, 0:HALF])
        bottom = small_inverse(diag[HALF:BLK, HALF:BLK])
        inv[0:HALF, 0:HALF] = top
        inv[0:HALF, HALF:BLK] = jnp.zeros((HALF, HALF), F32)
        inv[HALF:BLK, HALF:BLK] = bottom
        inv[HALF:BLK, 0:HALF] = -full(bottom, full(diag[HALF:BLK, 0:HALF], top))

    def part(ref, q):
        if PARTS == 1:
            return ref.at[q]
        return ref.at[lax.div(q, PARTS), pl.ds(pl.multiple_of(lax.rem(q, PARTS) * ROWS, ROWS), ROWS), :]

    def to_other(q):
        return remote(part(own, q), part(oth, q), oth_send.at[q], oth_recv.at[q], other)

    def down_ring(q, target, sem):
        return remote(
            part(own, q), part(own, q), own_send.at[sem, q], own_recv.at[q], (2 * target + k, c)
        )

    def forwards_ring(q):
        return ((z == 0) & (lax.rem(q, 2) == 0)) | ((z == 2) & (lax.rem(q, 2) == 1))

    def to_panel(q):
        return pltpu.make_async_copy(part(own, q), part(panel.at[source_panel], q), copy_sem.at[q])

    def solved_chunk(q):
        @pl.when(is_top)
        def _():
            @pl.when(k == 1)
            def _():
                to_other(q).wait_recv()

            @pl.when(lax.rem(q, PARTS) == PARTS - 1)
            def _():
                s = lax.div(q, PARTS)

                @pl.when(k == 1)
                def _():
                    slab[s] = slab[s] - full(lower[...], oth[s])

                own[s] = full(inv[...], slab[s])

        @pl.when(z < 3)
        def _():
            down_ring(q, 1, 0).wait_recv()

    def send_solved(q):
        @pl.when(is_source)
        def _():
            to_panel(q).start()

        to_other(q).start()

        @pl.when(is_top)
        def _():
            down_ring(q, 0, 0).start()
            down_ring(q, 2, 1).start()

        @pl.when(forwards_ring(q))
        def _():
            down_ring(q, 1, 0).start()

    def hops(kp, b, q):
        odd = lax.rem(kp + q, 2)
        x_active = (k == 1) | (dy == 2 * b)
        y_active = (k == 0) | (dx == kp)
        return (
            (x_active & ((dx == kp) | ((kp == 1) & (dx == 2))), right),
            (x_active & ((dx == kp) | ((kp == 0) & (dx == 3))), left),
            (
                y_active
                & (
                    (dy == 2 * b)
                    | ((odd == 0) & (dy == 1) & (b == 0))
                    | ((odd == 1) & (dy == 3) & (b == 1))
                ),
                up,
            ),
            (
                y_active
                & (
                    (dy == 2 * b)
                    | ((odd == 0) & (dy == 1) & (b == 1))
                    | ((odd == 1) & (dy == 3) & (b == 0))
                ),
                down,
            ),
        )

    def hop(src, p, q, i, device):
        return remote(
            part(src, q), part(panel.at[p], q), dir_send.at[i, p, q], panel_recv.at[p, q], device
        )

    def to_cross(src, b, q):
        return remote(
            part(src, q), part(cross.at[b], q), cross_send.at[b, q], cross_recv.at[b, q], other
        )

    def start_all(src, kp, b, q):
        for i, (go, device) in enumerate(hops(kp, b, q)):
            @pl.when(go)
            def _(i=i, device=device):
                hop(src, 2 * kp + b, q, i, device).start()

        @pl.when(kp != k)
        def _():
            to_cross(src, b, q).start()

    def distance(kp, b):
        ex = lax.rem(dx + 4 - kp, 4)
        ey = lax.rem(dy + 4 - 2 * b, 4)
        return jnp.minimum(ex, 4 - ex) + jnp.minimum(ey, 4 - ey)

    def pass_on(kp, b, t):
        far = distance(kp, b)
        q = t - LAG * far

        @pl.when((far > 0) & (q >= 0) & (q < NQ))
        def _():
            p = 2 * kp + b
            hop(panel.at[p], p, q, 0, right).wait_recv()
            start_all(panel.at[p], kp, b, q)

    def staged(i, s):
        slot = i & 1
        return pltpu.make_async_copy(
            stage.at[slot, s], gram_ref.at[i, :, s, 0, :], stage_sem.at[slot, s]
        )

    def split_columns():
        @pl.when(jnp.logical_not(is_top & (k == 1)))
        def _():
            for q in range(NQ):
                to_other(q).wait_recv()

        for s in range(8):
            at = slice(HALF * s, HALF * (s + 1))
            high[0:BLK, at], low[0:BLK, at] = split(own[s])
            high[BLK:, at], low[BLK:, at] = split(oth[s])

    def gram_block(j, b):
        i = 2 * j + b
        p = 2 * k + b
        for n in range(2 * PARTS):
            to_cross(own, b, 2 * PARTS * j + n).wait_recv()
        mine = jnp.concatenate([panel[p, 2 * j], panel[p, 2 * j + 1]], axis=1)
        theirs = jnp.concatenate([cross[b, 2 * j], cross[b, 2 * j + 1]], axis=1)
        a_high, a_low = split(jnp.concatenate([mine, theirs], axis=0))

        @pl.when(i >= 2)
        def _():
            for s in range(8):
                staged(i, s).wait()

        for q in range(4):
            at = slice(BLK * q, BLK * (q + 1))
            b_high, b_low = high[:, at], low[:, at]
            value = (tdot(a_low, b_high) + tdot(a_high, b_low)) + tdot(a_high, b_high)
            value = value * SCALE
            stage[i & 1, 2 * q] = value[:, :HALF]
            stage[i & 1, 2 * q + 1] = value[:, HALF:]
            staged(i, 2 * q).start()
            staged(i, 2 * q + 1).start()

    def step(t, carry):
        @pl.when(t < NQ)
        def _():
            solved_chunk(t)

            @pl.when(is_source)
            def _():
                start_all(own, lax.rem(c, 2), lax.div(c, 8), t)

            send_solved(t)

        for kp in range(2):
            for b in range(2):
                pass_on(kp, b, t)

        def start_late(m, carry):
            start_finished(m, False)
            return carry

        first = EARLY + PACE * (t - AFTER)
        lax.fori_loop(
            jnp.where(t < AFTER, 28, jnp.minimum(first, 28)),
            jnp.where(t == STEPS - 1, 28, jnp.minimum(first + PACE, 28)),
            start_late,
            0,
        )
        return carry

    lax.fori_loop(0, STEPS, step, 0)

    @pl.when(is_source)
    def _():
        for q in range(NQ):
            to_panel(q).wait()

    split_columns()
    last = [
        pltpu.make_async_copy(
            own.at[r], fin_ref.at[SLOT, 6 + k, :, 0, :], local_sem.at[2]
        ),
        pltpu.make_async_copy(
            oth.at[r], fin_ref.at[SLOT, 7 - k, :, 0, :], local_sem.at[3]
        ),
    ]
    for copy in last:
        copy.start()

    def product(j, carry):
        gram_block(j, 0)
        gram_block(j, 1)
        return carry

    lax.fori_loop(0, 4, product, 0)

    for i in (6, 7):
        for s in range(8):
            staged(i, s).wait()
    for copy in last:
        copy.wait()
    own_rows.wait()

    @pl.when(z < 3)
    def _():
        own_last.wait()

    def close(q, carry):
        to_other(q).wait_send()

        @pl.when(is_top)
        def _():
            down_ring(q, 0, 0).wait_send()
            down_ring(q, 2, 1).wait_send()

        @pl.when(forwards_ring(q))
        def _():
            down_ring(q, 1, 0).wait_send()

        for kp in range(2):
            for b in range(2):
                for i, (go, device) in enumerate(hops(kp, b, q)):
                    @pl.when(go)
                    def _(i=i, p=2 * kp + b, device=device):
                        hop(panel.at[p], p, q, i, device).wait_send()
        for b in range(2):
            to_cross(own, b, q).wait_send()
        return carry

    lax.fori_loop(0, NQ, close, 0)

    def close_finished(m, carry):
        go, copy = finished(m, False)

        @pl.when(go)
        def _():
            copy.wait_send()

        go, copy = finished(m, True)

        @pl.when(go)
        def _():
            copy.wait_recv()

        return carry

    lax.fori_loop(0, 28, close_finished, 0)


def per_device(working, factor_panel):
    dma = pltpu.SemaphoreType.DMA
    gram, finished = pl.pallas_call(
        kernel,
        out_shape=[
            pltpu.VMEM((8, BLK, 8, 1, HALF), F32),
            pltpu.VMEM((4, 8, BLK, 1, HALF), F32),
        ],
        in_specs=[pl.BlockSpec(memory_space=pl.ANY)] * 2,
        out_specs=[pl.BlockSpec(memory_space=pltpu.VMEM)] * 2,
        scratch_shapes=[
            pltpu.VMEM((8, BLK, HALF), F32),
            pltpu.VMEM((8, BLK, HALF), F32),
            pltpu.VMEM((4, 8, BLK, HALF), F32),
            pltpu.VMEM((2, 8, BLK, HALF), F32),
            pltpu.VMEM((2 * BLK, 8 * HALF), BF16),
            pltpu.VMEM((2 * BLK, 8 * HALF), BF16),
            pltpu.VMEM((2, 8, BLK, HALF), F32),
            pltpu.VMEM((8, BLK, HALF), F32),
            pltpu.VMEM((BLK, BLK), F32),
            pltpu.VMEM((BLK, BLK), F32),
            pltpu.VMEM((BLK, BLK), F32),
            dma((10,)),
            dma((28,)), dma((28,)),
            dma((4,)),
            dma((NQ,)), dma((NQ,)),
            dma((2, NQ)), dma((NQ,)),
            dma((NQ,)),
            dma((4, 4, NQ)), dma((4, NQ)),
            dma((2, NQ)), dma((2, NQ)),
            dma((2, 8)),
        ],
        compiler_params=pltpu.CompilerParams(
            collective_id=0, has_side_effects=True, vmem_limit_bytes=44 * 2**20
        ),
        cost_estimate=pl.CostEstimate(
            flops=3 * 2**31, bytes_accessed=20 * 2**20, transcendentals=0
        ),
        name="window",
    )(working.reshape(8, BLK, 8, 1, HALF), factor_panel)
    return gram.reshape(8, 1, BLK, 4, 1, BLK), finished.reshape(4, 8, BLK, 1, 1, HALF)


def solution(mesh):
    placed = (P(None, "row", None, None, "col", None), P(None, None, "row", None, None))
    return jax.shard_map(
        per_device,
        mesh=mesh,
        in_specs=placed,
        out_specs=(
            P(None, "row", None, None, "col", None),
            P(None, None, None, "col", "row", None),
        ),
        check_vma=False,
    )
```
